32 devices in a mesh: ctx: 8 (over z, y), tp: 4 (over x, core).
Axes of the slice: x: 2, y: 2, z: 4, core: 2. Of those that a mesh axis runs over, the one named last changes fastest.
Arguments:
- inputs: bfloat16 [4096, 1024], P('ctx'), may hold values from -6 to 6
- cotangent: bfloat16 [4096, 1024], P('ctx'), may hold values from -6 to 6
- positions: int32 [4096], replicated, may hold values from 0 to 2047, as said below
- first_gain: float32 [1024], replicated, may hold values from 0.1 to 1.9
- first_shift: float32 [1024], replicated, may hold values from -1.75 to 1.75
- second_gain: float32 [1024], replicated, may hold values from 0.1 to 1.9
- second_shift: float32 [1024], replicated, may hold values from -1.75 to 1.75
- qkv_weight: bfloat16 [1024, 3, 1024], P(None, None, 'tp'), may hold values from -0.1875 to 0.1875
- qkv_bias: float32 [3, 1024], P(None, 'tp'), may hold values from -1.75 to 1.75
- dense_weight: bfloat16 [1024, 1024], P('tp'), may hold values from -1.75 to 1.75
- dense_bias: float32 [1024], replicated, may hold values from -1.75 to 1.75
- up_weight: bfloat16 [1024, 4096], P(None, 'tp'), may hold values from -0.1875 to 0.1875
- up_bias: float32 [4096], P('tp'), may hold values from -1.75 to 1.75
- down_weight: bfloat16 [4096, 1024], P('tp'), may hold values from -0.09375 to 0.09375
- down_bias: float32 [1024], replicated, may hold values from -1.75 to 1.75
Outputs:
- output: bfloat16 [4096, 1024], P('ctx', 'tp')
- input_grad: float32 [4096, 1024], P('ctx', 'tp')
- first_gain_grad: float32 [1024], P('tp')
- first_shift_grad: float32 [1024], P('tp')
- second_gain_grad: float32 [1024], P('tp')
- second_shift_grad: float32 [1024], P('tp')
- qkv_weight_grad: float32 [1024, 3, 1024], P(None, None, 'tp')
- qkv_bias_grad: float32 [3, 1024], P(None, 'tp')
- dense_weight_grad: float32 [1024, 1024], P('tp')
- dense_bias_grad: float32 [1024], replicated
- up_weight_grad: float32 [1024, 4096], P(None, 'tp')
- up_bias_grad: float32 [4096], P('tp')
- down_weight_grad: float32 [4096, 1024], P('tp')
- down_bias_grad: float32 [1024], replicated
The draws below stay inside these ranges and needn't reach their ends.
Inputs may be any that keep to these rules, and one draw needn't show every extreme that they name: Each sequence's 2048 positions appear once. Cut each sequence into 16 blocks of 128 consecutive positions, numbered 0 to 15. On each index of ctx, the 256 rows of a sequence are two runs of 128 rows, each run one whole block in increasing order: block p and block 15 - p, in either order, with p below 8 and different on every index of ctx.
All inputs are finite; a program needn't handle non-finite values.
Results may differ from the reference program's by a relative error of at most 0.025.
Values may be sent and summed in bfloat16 or wider, within the bound.
A program may use at most 320 MiB of HBM per device.

```python
import jax
import jax.numpy as jnp
from jax import lax

D = 1024
H = 16
HD = 64
ROT = 16
FF = 4096
SEQS = 2
TOK_SEQ = 256
SEQ_LEN = 2048
TOKENS = 4096
N_CTX = 8


def draw_positions(key, part):
    key = jax.random.fold_in(key, 11)
    order_key = jax.random.fold_in(key, 1)
    flip_key = jax.random.fold_in(key, 2)
    half_len = TOK_SEQ // 2
    orders = jax.vmap(lambda one_key: jax.random.permutation(one_key, N_CTX))(jax.random.split(order_key, SEQS))
    orders = orders.astype(jnp.int32)
    flips = jax.random.randint(flip_key, (SEQS, N_CTX), 0, 2, dtype=jnp.int32)
    mirror = 2 * N_CTX - 1 - orders
    first_block = jnp.where(flips == 1, mirror, orders)
    second_block = jnp.where(flips == 1, orders, mirror)
    offsets = jnp.arange(half_len, dtype=jnp.int32)
    placed = jnp.concatenate([first_block[..., None] * half_len + offsets, second_block[..., None] * half_len + offsets], axis=-1)
    return jnp.transpose(placed, (1, 0, 2)).reshape(TOKENS).astype(jnp.int32)


def steps_of(own_key, dims, cuts, least, largest):
    gain, own = 1.0, jax.random.fold_in(own_key, 6)
    for axis_at, shards_of in cuts:
        draws = jnp.exp(jax.random.uniform(jax.random.fold_in(own, axis_at), (shards_of,), jnp.float32, least / len(cuts), largest / len(cuts)))
        gain = gain * jnp.repeat(draws, dims[axis_at] // shards_of).reshape([-1 if axis == axis_at else 1 for axis in range(len(dims))])
    return gain


def centred(stream_key, dims, deviation, reach, cuts=(), kind=jnp.bfloat16):
    result = jax.random.normal(stream_key, dims, jnp.float32) * deviation
    if len(cuts) > 0:
        result = steps_of(stream_key, dims, cuts, -0.22, 0.18) * result
    return jnp.clip(result, min=-reach, max=reach).astype(kind)


def setup_inputs(seed: int = 0) -> dict:
    key_of = jax.random.split(jax.random.key(seed), 16)
    inputs = centred(key_of[0], (TOKENS, D), 1.0, 6.0, ((0, 8),))
    cotangent = centred(key_of[1], (TOKENS, D), 1.0, 6.0, ((0, 8),))
    positions = draw_positions(jax.random.fold_in(key_of[15], 71), 0)
    first_gain = jnp.clip(1.0 + 0.18 * jax.random.normal(key_of[3], (D,), jnp.float32), 0.1, 1.9)
    first_shift = centred(key_of[4], (D,), 0.3, 1.75, (), jnp.float32)
    second_gain = jnp.clip(1.0 + 0.18 * jax.random.normal(key_of[5], (D,), jnp.float32), 0.1, 1.9)
    second_shift = centred(key_of[6], (D,), 0.3, 1.75, (), jnp.float32)
    qkv_weight = centred(key_of[7], (D, 3, D), D ** -0.5, 0.1875, ((2, 4),))
    qkv_bias = centred(key_of[8], (3, D), 0.3, 1.75, ((1, 4),), jnp.float32)
    dense_weight = centred(key_of[9], (D, D), (0.006 * SEQ_LEN ** 0.5), 1.75, ((0, 4),))
    dense_bias = centred(key_of[10], (D,), 0.3, 1.75, (), jnp.float32)
    up_weight = centred(key_of[11], (D, FF), D ** -0.5, 0.1875, ((1, 4),))
    up_bias = centred(key_of[12], (FF,), 0.3, 1.75, ((0, 4),), jnp.float32)
    down_weight = centred(key_of[13], (FF, D), FF ** -0.5, 0.09375, ((0, 4),))
    down_bias = centred(key_of[14], (D,), 0.3, 1.75, (), jnp.float32)
    return dict(inputs=inputs, cotangent=cotangent, positions=positions, first_gain=first_gain, first_shift=first_shift, second_gain=second_gain, second_shift=second_shift, qkv_weight=qkv_weight, qkv_bias=qkv_bias, dense_weight=dense_weight, dense_bias=dense_bias, up_weight=up_weight, up_bias=up_bias, down_weight=down_weight, down_bias=down_bias)


EPSILON = 1e-05
ROPE_BASE = 10000.0
MASKED_SCORE = -1e+30
HIGHEST = lax.Precision.HIGHEST

@jax.custom_vjp
def low(v):
    return lax.optimization_barrier(v.astype(jnp.bfloat16)).astype(jnp.float32)

@jax.custom_vjp
def low_back(v):
    return v

def low_keep(v):
    return (low(v), None)

def low_pass(kept, grad):
    return (grad,)

def back_keep(v):
    return (v, None)

def back_low(kept, grad):
    return (low(grad),)
low.defvjp(low_keep, low_pass)
low_back.defvjp(back_keep, back_low)

def layer_norm(values, norm_gain, norm_shift):
    centered = values - lax.optimization_barrier(jnp.mean(values, axis=-1, keepdims=True))
    spread = lax.optimization_barrier(jnp.mean(centered * centered, axis=-1, keepdims=True))
    return centered * lax.rsqrt(spread + EPSILON) * norm_gain + norm_shift

def rotate(values, places, rot_dims):
    half_rot = rot_dims // 2
    freq_index = jnp.arange(half_rot, dtype=jnp.float32)
    inverse = ROPE_BASE ** (-2.0 * freq_index / rot_dims)
    angles = places.astype(jnp.float32)[..., None] * inverse
    cosine = jnp.cos(angles)[..., None, :]
    sine_term = jnp.sin(angles)[..., None, :]
    first_half = values[..., :half_rot]
    second_half = values[..., half_rot:rot_dims]
    return jnp.concatenate([first_half * cosine - second_half * sine_term, second_half * cosine + first_half * sine_term, values[..., rot_dims:]], axis=-1)

def attend_block(query_blk, query_pos, key_rows, value_rows, key_pos):
    scores = jnp.einsum('qhe,khe->hqk', query_blk, key_rows, precision=HIGHEST) * HD ** (-0.5)
    scores = low_back(scores)
    allowed = key_pos[None, None, :] <= query_pos[None, :, None]
    masked = jnp.where(allowed, scores, MASKED_SCORE)
    row_top = lax.optimization_barrier(jnp.max(masked, axis=-1, keepdims=True))
    exp_terms = jnp.where(allowed, jnp.exp(masked - row_top), 0.0)
    row_total = lax.optimization_barrier(jnp.sum(exp_terms, axis=-1))
    numerator = low_back(jnp.einsum('hqk,khe->qhe', low(exp_terms), value_rows, precision=HIGHEST))
    return low(numerator / jnp.transpose(row_total)[:, :, None])

def attend_sequence(queries, key_rows, value_rows, places):
    query_len = min(512, SEQ_LEN)

    def one_block(block_pair):
        return attend_block(block_pair[0], block_pair[1], key_rows, value_rows, places)
    grouped = lax.map(jax.checkpoint(one_block), (queries.reshape(SEQ_LEN // query_len, query_len, H, HD), places.reshape(SEQ_LEN // query_len, query_len)))
    return grouped.reshape(SEQ_LEN, H * HD)

def reference(inputs, cotangent, positions, first_gain, first_shift, second_gain, second_shift, qkv_weight, qkv_bias, dense_weight, dense_bias, up_weight, up_bias, down_weight, down_bias):
    seq_places = positions.reshape(N_CTX, SEQS, TOK_SEQ).transpose(1, 0, 2).reshape(SEQS, SEQ_LEN)

    def layer_forward(input_rows, gain_one, shift_one, gain_two, shift_two, qkv_w, qkv_b, dense_w, dense_b, up_w, up_b, down_w, down_b):
        normed_one = low(layer_norm(input_rows, gain_one, shift_one))
        normed_two = low(layer_norm(input_rows, gain_two, shift_two))
        qkv_mixed = low_back(jnp.einsum('td,dce->tce', normed_one, qkv_w, precision=HIGHEST) + qkv_b)
        by_seq = qkv_mixed.reshape(N_CTX, SEQS, TOK_SEQ, 3, H, HD).transpose(1, 0, 2, 3, 4, 5)
        by_seq = by_seq.reshape(SEQS, SEQ_LEN, 3, H, HD)
        queries = low(rotate(by_seq[:, :, 0], seq_places, ROT))
        keys_all = low(rotate(by_seq[:, :, 1], seq_places, ROT))
        values_all = low(by_seq[:, :, 2])
        attended = jnp.stack([attend_sequence(queries[seq_number], keys_all[seq_number], values_all[seq_number], seq_places[seq_number]) for seq_number in range(SEQS)])
        attended_rows = attended.reshape(SEQS, N_CTX, TOK_SEQ, D).transpose(1, 0, 2, 3).reshape(TOKENS, D)
        dense_out = jnp.dot(attended_rows, dense_w, precision=HIGHEST) + dense_b
        up_proj = low_back(jnp.dot(normed_two, up_w, precision=HIGHEST) + up_b)
        activated = low(jax.nn.gelu(up_proj, approximate=False))
        return input_rows + dense_out + jnp.dot(activated, down_w, precision=HIGHEST) + down_b
    output, pull_back = jax.vjp(layer_forward, inputs.astype(jnp.float32), first_gain.astype(jnp.float32), first_shift.astype(jnp.float32), second_gain.astype(jnp.float32), second_shift.astype(jnp.float32), qkv_weight.astype(jnp.float32), qkv_bias.astype(jnp.float32), dense_weight.astype(jnp.float32), dense_bias.astype(jnp.float32), up_weight.astype(jnp.float32), up_bias.astype(jnp.float32), down_weight.astype(jnp.float32), down_bias.astype(jnp.float32))
    grads = pull_back(cotangent.astype(jnp.float32))
    return (output.astype(jnp.bfloat16), grads[0], grads[1], grads[2], grads[3], grads[4], grads[5], grads[6], grads[7], grads[8], grads[9], grads[10], grads[11], grads[12])
```

```python
from functools import partial

import jax
import jax.numpy as jnp
from jax import lax
from jax.experimental import pallas as pl
from jax.experimental.pallas import tpu as pltpu
from jax.sharding import PartitionSpec as P

HD = 64
ROT = 16
SEQS = 2
RUN = 128
TILE = 256


EPSILON = 1e-05
ROPE_BASE = 10000.0
MASKED_SCORE = -1e30


def layer_norm(values, norm_gain, norm_shift):
    centered = values - jnp.mean(values, axis=-1, keepdims=True)
    spread = jnp.mean(centered * centered, axis=-1, keepdims=True)
    return centered * lax.rsqrt(spread + EPSILON) * norm_gain + norm_shift


def rotate(values, places, rot_dims):
    half_rot = rot_dims // 2
    freq_index = jnp.arange(half_rot, dtype=jnp.float32)
    inverse = ROPE_BASE ** (-2.0 * freq_index / rot_dims)
    angles = places.astype(jnp.float32)[..., None] * inverse
    cosine = jnp.cos(angles)[..., None, :]
    sine_term = jnp.sin(angles)[..., None, :]
    first_half = values[..., :half_rot]
    second_half = values[..., half_rot:rot_dims]
    return jnp.concatenate(
        [
            first_half * cosine - second_half * sine_term,
            second_half * cosine + first_half * sine_term,
            values[..., rot_dims:],
        ],
        axis=-1,
    )


def contract_rows(left_side, right_side):
    return lax.dot_general(
        left_side, right_side, (((0,), (0,)), ((), ())), preferred_element_type=jnp.float32
    )


def contract_cols(left_side, right_side):
    return lax.dot_general(
        left_side, right_side, (((1,), (1,)), ((), ())), preferred_element_type=jnp.float32
    )


def block_scores(queries, key_rows, query_places, key_places, score_scale):
    scores = (
        jnp.einsum("sqhe,skhe->shqk", queries, key_rows, preferred_element_type=jnp.float32)
        * score_scale
    )
    allowed = key_places[:, None, None, :] <= query_places[:, None, :, None]
    return (jnp.where(allowed, scores, MASKED_SCORE), allowed)


def block_grads(
    queries, key_rows, value_rows, query_places, key_places, row_top, row_corr, d_numer, score_scale
):
    masked, allowed = block_scores(queries, key_rows, query_places, key_places, score_scale)
    exp_terms = jnp.where(allowed, jnp.exp(masked - row_top[..., None]), 0.0)
    along_value = jnp.einsum(
        "sqhe,skhe->shqk", d_numer, value_rows, preferred_element_type=jnp.float32
    )
    d_score = (exp_terms * (along_value - row_corr[..., None])).astype(jnp.bfloat16)
    return (exp_terms.astype(jnp.bfloat16), d_score)


def spread_attention(
    queries, key_own, value_own, d_att, own_places, all_places, block_len, block_count, score_scale
):
    _, tok_seq, heads_here, _ = queries.shape
    seq_len = all_places.shape[1]
    local_width = heads_here * HD
    tok_dev = SEQS * tok_seq
    key_all, value_all = (
        lax.all_gather(key_own.reshape(SEQS, tok_seq, local_width), "ctx", axis=1, tiled=True),
        lax.all_gather(value_own.reshape(SEQS, tok_seq, local_width), "ctx", axis=1, tiled=True),
    )

    def key_slice(block_index):
        offset = block_index * block_len
        key_rows = lax.dynamic_slice_in_dim(key_all, offset, block_len, 1).reshape(
            SEQS, block_len, heads_here, HD
        )
        value_rows = lax.dynamic_slice_in_dim(value_all, offset, block_len, 1).reshape(
            SEQS, block_len, heads_here, HD
        )
        key_places = lax.dynamic_slice_in_dim(all_places, offset, block_len, 1)
        return (key_rows, value_rows, key_places)

    def find_top(block_index, running):
        key_rows, value_rows, key_places = key_slice(block_index)
        masked, allowed = block_scores(queries, key_rows, own_places, key_places, score_scale)
        return jnp.maximum(running, jnp.max(masked, axis=-1))

    row_top = lax.fori_loop(
        0, block_count, find_top, jnp.full((SEQS, heads_here, tok_seq), MASKED_SCORE, jnp.float32)
    )

    def add_block(block_index, carried):
        row_total, numerator = carried
        key_rows, value_rows, key_places = key_slice(block_index)
        masked, allowed = block_scores(queries, key_rows, own_places, key_places, score_scale)
        exp_terms = jnp.where(allowed, jnp.exp(masked - row_top[..., None]), 0.0)
        numerator = numerator + jnp.einsum(
            "shqk,skhe->sqhe",
            exp_terms.astype(jnp.bfloat16),
            value_rows,
            preferred_element_type=jnp.float32,
        )
        return (row_total + jnp.sum(exp_terms, axis=-1), numerator)

    zeros_q = jnp.zeros((SEQS, tok_seq, heads_here, HD), jnp.float32)
    row_total, numerator = lax.fori_loop(
        0, block_count, add_block, (jnp.zeros((SEQS, heads_here, tok_seq), jnp.float32), zeros_q)
    )
    total_rows = jnp.transpose(row_total, (0, 2, 1))[..., None]
    attended = (numerator / total_rows).astype(jnp.bfloat16).reshape(tok_dev, local_width)
    d_numer = (d_att / total_rows).astype(jnp.bfloat16)
    row_corr = jnp.transpose(jnp.sum(d_att * numerator, axis=-1), (0, 2, 1)) / (
        row_total * row_total
    )

    def full_grad(block_index, carried):
        d_query, d_keys, d_values = carried
        key_rows, value_rows, key_places = key_slice(block_index)
        weights, d_score = block_grads(
            queries,
            key_rows,
            value_rows,
            own_places,
            key_places,
            row_top,
            row_corr,
            d_numer,
            score_scale,
        )
        d_query = d_query + jnp.einsum(
            "shqk,skhe->sqhe", d_score, key_rows, preferred_element_type=jnp.float32
        )
        key_part = jnp.einsum(
            "shqk,sqhe->skhe", d_score, queries, preferred_element_type=jnp.float32
        ).reshape(SEQS, block_len, local_width)
        value_part = jnp.einsum(
            "shqk,sqhe->skhe", weights, d_numer, preferred_element_type=jnp.float32
        ).reshape(SEQS, block_len, local_width)
        d_keys = lax.dynamic_update_slice_in_dim(d_keys, key_part, block_index * block_len, 1)
        d_values = lax.dynamic_update_slice_in_dim(d_values, value_part, block_index * block_len, 1)
        return (d_query, d_keys, d_values)

    full_zeros = jnp.zeros((SEQS, seq_len, local_width), jnp.float32)
    d_query, d_keys, d_values = lax.fori_loop(
        0, block_count, full_grad, (zeros_q, full_zeros, full_zeros)
    )
    d_key_own, d_value_own = (
        lax.psum_scatter(d_keys, "ctx", scatter_dimension=1, tiled=True),
        lax.psum_scatter(d_values, "ctx", scatter_dimension=1, tiled=True),
    )
    grad_shape = (SEQS, tok_seq, heads_here, HD)
    return (
        attended,
        d_query * score_scale,
        d_key_own.reshape(grad_shape) * score_scale,
        d_value_own.reshape(grad_shape),
    )


def head_kernel(score_scale, table, x_ref, y_ref, sorted_rows, turned, key_value, sorted_out):
    length = x_ref.shape[0]
    for run in range(length // RUN):
        place = pl.multiple_of(table[run] * RUN, RUN)
        sorted_rows[pl.ds(place, RUN), :] = x_ref[run * RUN : (run + 1) * RUN, :]
    for start in range(0, length, TILE):
        chunk = sorted_rows[start : start + TILE, :].astype(jnp.float32)
        turned[:, start : start + TILE] = chunk.T.astype(jnp.bfloat16)
    key_value[...] = jnp.zeros_like(key_value)

    def multiply(left_side, right_side):
        return jnp.dot(left_side, right_side, preferred_element_type=jnp.float32)

    key_index = lax.broadcasted_iota(jnp.int32, (TILE, TILE), 0)
    query_index = lax.broadcasted_iota(jnp.int32, (TILE, TILE), 1)
    allowed = key_index <= query_index
    for start in range(0, length, TILE):
        width = start + TILE
        tile = slice(start, width)
        query_tile = sorted_rows[tile, :HD]
        key_rows = sorted_rows[:width, HD : 2 * HD]
        value_rows = sorted_rows[:width, 2 * HD : 3 * HD]
        scores = multiply(key_rows, turned[:HD, tile])
        edge = jnp.where(allowed, scores[start:, :], MASKED_SCORE)
        scores = edge if start == 0 else jnp.concatenate([scores[:start, :], edge], axis=0)
        top = jnp.max(scores, axis=0, keepdims=True)
        exp_terms = jnp.exp(scores - top)
        total = jnp.sum(exp_terms, axis=0, keepdims=True)
        weights = exp_terms.astype(jnp.bfloat16)
        numerator = multiply(turned[2 * HD : 3 * HD, :width], weights)
        d_att = turned[3 * HD :, tile].astype(jnp.float32)
        d_numer = d_att / total
        corr = jnp.sum(d_att * numerator, axis=0, keepdims=True) / (total * total)
        along_value = multiply(value_rows, d_numer.astype(jnp.bfloat16))
        d_score = (exp_terms * (along_value - corr)).astype(jnp.bfloat16)
        d_query = multiply(turned[HD : 2 * HD, :width], d_score) * score_scale
        both = jnp.concatenate([d_query, numerator / total], axis=0)
        sorted_out[tile, : 2 * HD] = both.T.astype(jnp.bfloat16)
        key_value[:width, :HD] += multiply(d_score, query_tile)
        key_value[:width, HD:] += multiply(weights, d_numer.T.astype(jnp.bfloat16))
    sorted_out[:, 2 * HD :] = key_value[...].astype(jnp.bfloat16)
    for run in range(length // RUN):
        place = pl.multiple_of(table[run] * RUN, RUN)
        y_ref[run * RUN : (run + 1) * RUN, :] = sorted_out[pl.ds(place, RUN), :]


def head_attention(packed, table, score_scale):
    length, width = packed.shape
    pairs = length * length // 2
    return pl.pallas_call(
        partial(head_kernel, score_scale),
        out_shape=jax.ShapeDtypeStruct((length, width), jnp.bfloat16),
        in_specs=[
            pl.BlockSpec(memory_space=pltpu.SMEM),
            pl.BlockSpec(memory_space=pltpu.VMEM),
        ],
        out_specs=pl.BlockSpec(memory_space=pltpu.VMEM),
        scratch_shapes=[
            pltpu.VMEM((length, width), jnp.bfloat16),
            pltpu.VMEM((width, length), jnp.bfloat16),
            pltpu.VMEM((length, 2 * HD), jnp.float32),
            pltpu.VMEM((length, width), jnp.bfloat16),
        ],
        compiler_params=pltpu.CompilerParams(vmem_limit_bytes=48 * 1024 * 1024),
        cost_estimate=pl.CostEstimate(
            flops=12 * pairs * HD, bytes_accessed=4 * length * width, transcendentals=pairs
        ),
    )(table, packed)


def swap_with(array, bit, count):
    return lax.ppermute(array, "ctx", [(index, index ^ bit) for index in range(count)])


def sum_over_ctx(partial_sum, bits):
    count = lax.axis_size("ctx")
    here = lax.axis_index("ctx")
    held = partial_sum
    for bit in bits:
        half = held.shape[0] // 2
        side = jnp.where((here & bit) != 0, 1, 0)
        sent = lax.dynamic_slice_in_dim(held, (1 - side) * half, half, 0).astype(jnp.bfloat16)
        kept = lax.dynamic_slice_in_dim(held, side * half, half, 0)
        held = kept + swap_with(sent, bit, count).astype(jnp.float32)
    held = held.astype(jnp.bfloat16)
    for bit in reversed(bits):
        other = swap_with(held, bit, count)
        upper = (here & bit) != 0
        held = jnp.concatenate(
            [jnp.where(upper, other, held), jnp.where(upper, held, other)], axis=0
        )
    return held.astype(jnp.float32)


def bit_orders(count):
    bits = []
    while 1 << len(bits) < count:
        bits.append(1 << len(bits))
    return (bits, bits[1:2] + bits[:1] + bits[2:])


def local(
    inputs,
    cotangent,
    positions,
    first_gain,
    first_shift,
    second_gain,
    second_shift,
    qkv_weight,
    qkv_bias,
    dense_weight,
    dense_bias,
    up_weight,
    up_bias,
    down_weight,
    down_bias,
):
    ctx_count = lax.axis_size("ctx")
    tp_count = lax.axis_size("tp")
    ctx_here = lax.axis_index("ctx")
    tp_here = lax.axis_index("tp")
    tok_dev, model_width = inputs.shape
    tok_seq = tok_dev // SEQS
    local_width = dense_weight.shape[0]
    heads_here = local_width // HD
    seq_len = tok_seq * ctx_count
    block_len = min(2048, seq_len)
    block_count = seq_len // block_len
    score_scale = HD ** (-0.5)
    col_count = model_width // tp_count
    place_grid = positions.reshape(ctx_count, SEQS, tok_seq)
    own_places = lax.dynamic_index_in_dim(place_grid, ctx_here, 0, keepdims=False)
    all_places = jnp.transpose(place_grid, (1, 0, 2)).reshape(SEQS, seq_len)

    def take_cols(array):
        return lax.dynamic_slice_in_dim(array, tp_here * col_count, col_count, array.ndim - 1)

    input_rows = inputs.astype(jnp.float32)
    normed_one = layer_norm(input_rows, first_gain, first_shift).astype(jnp.bfloat16)
    normed_two = layer_norm(input_rows, second_gain, second_shift).astype(jnp.bfloat16)
    qkv_mixed = (
        jnp.einsum("td,dce->tce", normed_one, qkv_weight, preferred_element_type=jnp.float32)
        + qkv_bias
    )
    qkv_split = qkv_mixed.reshape(SEQS, tok_seq, 3, heads_here, HD)
    queries = rotate(qkv_split[:, :, 0], own_places, ROT).astype(jnp.bfloat16)
    key_own = rotate(qkv_split[:, :, 1], own_places, ROT).astype(jnp.bfloat16)
    value_own = qkv_split[:, :, 2].astype(jnp.bfloat16)
    d_att = contract_cols(cotangent, dense_weight).reshape(SEQS, tok_seq, heads_here, HD)
    up_proj = jnp.dot(normed_two, up_weight, preferred_element_type=jnp.float32) + up_bias
    activated = jax.nn.gelu(up_proj, approximate=False).astype(jnp.bfloat16)
    cot_rows = cotangent.astype(jnp.float32)
    gelu_pull = jax.vjp(partial(jax.nn.gelu, approximate=False), up_proj)[1]
    d_up = gelu_pull(contract_cols(cotangent, down_weight))[0].astype(jnp.bfloat16)
    orders = bit_orders(ctx_count)
    grad_down = sum_over_ctx(contract_rows(activated, cotangent), orders[0])
    grad_up = sum_over_ctx(contract_rows(normed_two, d_up), orders[1])
    grad_up_bias = jnp.sum(d_up.astype(jnp.float32), axis=0)
    d_two = contract_cols(d_up, up_weight)
    two_cols = lax.psum_scatter(
        d_two.astype(jnp.bfloat16), "tp", scatter_dimension=1, tiled=True
    ).astype(jnp.float32)

    if ctx_count == SEQS * heads_here and seq_len % TILE == 0 and tok_seq % RUN == 0:
        packed = jnp.stack(
            [
                (queries * score_scale).astype(jnp.bfloat16),
                key_own,
                value_own,
                d_att.astype(jnp.bfloat16),
            ],
            axis=3,
        )
        packed = jnp.transpose(packed, (0, 2, 1, 3, 4)).reshape(ctx_count, tok_seq, 4 * HD)
        packed = lax.all_to_all(packed, "ctx", 0, 0, tiled=True).reshape(seq_len, 4 * HD)
        starts = lax.dynamic_index_in_dim(place_grid, ctx_here // heads_here, 1, keepdims=False)
        table = starts.reshape(seq_len // RUN, RUN)[:, 0] // RUN
        grads = head_attention(packed, table, score_scale).reshape(ctx_count, tok_seq, 4 * HD)
        grads = lax.all_to_all(grads, "ctx", 0, 0, tiled=True)
        grads = grads.reshape(SEQS, heads_here, tok_seq, 4, HD)
        grads = jnp.transpose(grads, (3, 0, 2, 1, 4))
        attended = grads[1].reshape(tok_dev, local_width)
        d_query, d_key_own, d_value_own = (
            grads[0].astype(jnp.float32),
            grads[2].astype(jnp.float32),
            grads[3].astype(jnp.float32),
        )
    else:
        attended, d_query, d_key_own, d_value_own = spread_attention(
            queries,
            key_own,
            value_own,
            d_att,
            own_places,
            all_places,
            block_len,
            block_count,
            score_scale,
        )

    zeros_q = jnp.zeros((SEQS, tok_seq, heads_here, HD), jnp.float32)
    turn_back = jax.vjp(partial(rotate, places=own_places, rot_dims=ROT), zeros_q)[1]
    d_mixed = jnp.stack(
        [turn_back(d_query)[0], turn_back(d_key_own)[0], d_value_own], axis=2
    )
    d_mixed = d_mixed.reshape(tok_dev, 3, local_width).astype(jnp.bfloat16)
    grad_qkv = contract_rows(normed_one, d_mixed.reshape(tok_dev, 3 * local_width))
    grad_dense = contract_rows(cotangent, attended)
    joined = jnp.concatenate([grad_qkv, grad_dense], axis=1)
    middle = model_width // 2
    joined = jnp.concatenate(
        [sum_over_ctx(joined[:middle], orders[0]), sum_over_ctx(joined[middle:], orders[1])], axis=0
    )
    grad_qkv = joined[:, : 3 * local_width].reshape(model_width, 3, local_width)
    grad_dense = joined[:, 3 * local_width :].T
    grad_qkv_bias = jnp.sum(d_mixed.astype(jnp.float32), axis=0)
    d_one = jnp.einsum("tce,dce->td", d_mixed, qkv_weight, preferred_element_type=jnp.float32)
    partial_out = jnp.dot(attended, dense_weight, preferred_element_type=jnp.float32) + jnp.dot(
        activated, down_weight, preferred_element_type=jnp.float32
    )
    scattered = lax.psum_scatter(
        jnp.concatenate([partial_out, d_one], axis=0).astype(jnp.bfloat16),
        "tp",
        scatter_dimension=1,
        tiled=True,
    ).astype(jnp.float32)
    summed, one_cols = (scattered[:tok_dev], scattered[tok_dev:])
    output = (take_cols(input_rows) + summed + take_cols(dense_bias) + take_cols(down_bias)).astype(
        jnp.bfloat16
    )

    centered = input_rows - jnp.mean(input_rows, axis=-1, keepdims=True)
    inverse_spread = lax.rsqrt(jnp.mean(centered * centered, axis=-1, keepdims=True) + EPSILON)
    normalized = centered * inverse_spread
    scaled_one = d_one * first_gain
    scaled_two = d_two * second_gain
    means = lax.psum(
        jnp.stack(
            [
                jnp.mean(scaled_one + scaled_two, axis=-1),
                jnp.mean((scaled_one + scaled_two) * normalized, axis=-1),
            ]
        ),
        "tp",
    )
    cols = take_cols(normalized)
    scaled_cols = one_cols * take_cols(first_gain) + two_cols * take_cols(second_gain)
    d_rows = take_cols(cot_rows) + inverse_spread * (
        scaled_cols - means[0][:, None] - cols * means[1][:, None]
    )
    small = jnp.concatenate(
        [
            jnp.sum(one_cols * cols, axis=0),
            jnp.sum(one_cols, axis=0),
            jnp.sum(two_cols * cols, axis=0),
            jnp.sum(two_cols, axis=0),
            grad_qkv_bias.reshape(-1),
            jnp.sum(cot_rows, axis=0),
            grad_up_bias,
        ]
    )
    small = lax.psum(small, "ctx")
    gains = [small[index * col_count : (index + 1) * col_count] for index in range(4)]
    small = small[4 * col_count :]
    grad_qkv_bias = small[: 3 * local_width].reshape(3, local_width)
    small = small[3 * local_width :]
    bias_grad = small[:model_width]
    return (
        output,
        d_rows,
        *gains,
        grad_qkv,
        grad_qkv_bias,
        grad_dense,
        bias_grad,
        grad_up,
        small[model_width:],
        grad_down,
        bias_grad,
    )


def solution(mesh):
    in_specs = (
        P("ctx", None),
        P("ctx", None),
        P(),
        P(),
        P(),
        P(),
        P(),
        P(None, None, "tp"),
        P(None, "tp"),
        P("tp", None),
        P(),
        P(None, "tp"),
        P("tp"),
        P("tp", None),
        P(),
    )
    out_specs = (
        P("ctx", "tp"),
        P("ctx", "tp"),
        P("tp"),
        P("tp"),
        P("tp"),
        P("tp"),
        P(None, None, "tp"),
        P(None, "tp"),
        P("tp", None),
        P(),
        P(None, "tp"),
        P("tp"),
        P("tp", None),
        P(),
    )
    return jax.shard_map(local, mesh=mesh, in_specs=in_specs, out_specs=out_specs, check_vma=False)
```

```python
from functools import partial

import jax
import jax.numpy as jnp
from jax import lax
from jax.experimental import pallas as pl
from jax.experimental.pallas import tpu as pltpu
from jax.sharding import PartitionSpec as P

HD = 64
ROT = 16
SEQS = 2
RUN = 128
TILE = 256


EPSILON = 1e-05
ROPE_BASE = 10000.0
MASKED_SCORE = -1e30


def layer_norm(values, norm_gain, norm_shift):
    centered = values - jnp.mean(values, axis=-1, keepdims=True)
    spread = jnp.mean(centered * centered, axis=-1, keepdims=True)
    return centered * lax.rsqrt(spread + EPSILON) * norm_gain + norm_shift


def rotate(values, places, rot_dims):
    half_rot = rot_dims // 2
    freq_index = jnp.arange(half_rot, dtype=jnp.float32)
    inverse = ROPE_BASE ** (-2.0 * freq_index / rot_dims)
    angles = places.astype(jnp.float32)[..., None] * inverse
    cosine = jnp.cos(angles)[..., None, :]
    sine_term = jnp.sin(angles)[..., None, :]
    first_half = values[..., :half_rot]
    second_half = values[..., half_rot:rot_dims]
    return jnp.concatenate(
        [
            first_half * cosine - second_half * sine_term,
            second_half * cosine + first_half * sine_term,
            values[..., rot_dims:],
        ],
        axis=-1,
    )


def contract_rows(left_side, right_side):
    return lax.dot_general(
        left_side, right_side, (((0,), (0,)), ((), ())), preferred_element_type=jnp.float32
    )


def contract_cols(left_side, right_side):
    return lax.dot_general(
        left_side, right_side, (((1,), (1,)), ((), ())), preferred_element_type=jnp.float32
    )


def block_scores(queries, key_rows, query_places, key_places, score_scale):
    scores = (
        jnp.einsum("sqhe,skhe->shqk", queries, key_rows, preferred_element_type=jnp.float32)
        * score_scale
    )
    allowed = key_places[:, None, None, :] <= query_places[:, None, :, None]
    return (jnp.where(allowed, scores, MASKED_SCORE), allowed)


def block_grads(
    queries, key_rows, value_rows, query_places, key_places, row_top, row_corr, d_numer, score_scale
):
    masked, allowed = block_scores(queries, key_rows, query_places, key_places, score_scale)
    exp_terms = jnp.where(allowed, jnp.exp(masked - row_top[..., None]), 0.0)
    along_value = jnp.einsum(
        "sqhe,skhe->shqk", d_numer, value_rows, preferred_element_type=jnp.float32
    )
    d_score = (exp_terms * (along_value - row_corr[..., None])).astype(jnp.bfloat16)
    return (exp_terms.astype(jnp.bfloat16), d_score)


def spread_attention(
    queries, key_own, value_own, d_att, own_places, all_places, block_len, block_count, score_scale
):
    _, tok_seq, heads_here, _ = queries.shape
    seq_len = all_places.shape[1]
    local_width = heads_here * HD
    tok_dev = SEQS * tok_seq
    key_all, value_all = (
        lax.all_gather(key_own.reshape(SEQS, tok_seq, local_width), "ctx", axis=1, tiled=True),
        lax.all_gather(value_own.reshape(SEQS, tok_seq, local_width), "ctx", axis=1, tiled=True),
    )

    def key_slice(block_index):
        offset = block_index * block_len
        key_rows = lax.dynamic_slice_in_dim(key_all, offset, block_len, 1).reshape(
            SEQS, block_len, heads_here, HD
        )
        value_rows = lax.dynamic_slice_in_dim(value_all, offset, block_len, 1).reshape(
            SEQS, block_len, heads_here, HD
        )
        key_places = lax.dynamic_slice_in_dim(all_places, offset, block_len, 1)
        return (key_rows, value_rows, key_places)

    def find_top(block_index, running):
        key_rows, value_rows, key_places = key_slice(block_index)
        masked, allowed = block_scores(queries, key_rows, own_places, key_places, score_scale)
        return jnp.maximum(running, jnp.max(masked, axis=-1))

    row_top = lax.fori_loop(
        0, block_count, find_top, jnp.full((SEQS, heads_here, tok_seq), MASKED_SCORE, jnp.float32)
    )

    def add_block(block_index, carried):
        row_total, numerator = carried
        key_rows, value_rows, key_places = key_slice(block_index)
        masked, allowed = block_scores(queries, key_rows, own_places, key_places, score_scale)
        exp_terms = jnp.where(allowed, jnp.exp(masked - row_top[..., None]), 0.0)
        numerator = numerator + jnp.einsum(
            "shqk,skhe->sqhe",
            exp_terms.astype(jnp.bfloat16),
            value_rows,
            preferred_element_type=jnp.float32,
        )
        return (row_total + jnp.sum(exp_terms, axis=-1), numerator)

    zeros_q = jnp.zeros((SEQS, tok_seq, heads_here, HD), jnp.float32)
    row_total, numerator = lax.fori_loop(
        0, block_count, add_block, (jnp.zeros((SEQS, heads_here, tok_seq), jnp.float32), zeros_q)
    )
    total_rows = jnp.transpose(row_total, (0, 2, 1))[..., None]
    attended = (numerator / total_rows).astype(jnp.bfloat16).reshape(tok_dev, local_width)
    d_numer = (d_att / total_rows).astype(jnp.bfloat16)
    row_corr = jnp.transpose(jnp.sum(d_att * numerator, axis=-1), (0, 2, 1)) / (
        row_total * row_total
    )

    def full_grad(block_index, carried):
        d_query, d_keys, d_values = carried
        key_rows, value_rows, key_places = key_slice(block_index)
        weights, d_score = block_grads(
            queries,
            key_rows,
            value_rows,
            own_places,
            key_places,
            row_top,
            row_corr,
            d_numer,
            score_scale,
        )
        d_query = d_query + jnp.einsum(
            "shqk,skhe->sqhe", d_score, key_rows, preferred_element_type=jnp.float32
        )
        key_part = jnp.einsum(
            "shqk,sqhe->skhe", d_score, queries, preferred_element_type=jnp.float32
        ).reshape(SEQS, block_len, local_width)
        value_part = jnp.einsum(
            "shqk,sqhe->skhe", weights, d_numer, preferred_element_type=jnp.float32
        ).reshape(SEQS, block_len, local_width)
        d_keys = lax.dynamic_update_slice_in_dim(d_keys, key_part, block_index * block_len, 1)
        d_values = lax.dynamic_update_slice_in_dim(d_values, value_part, block_index * block_len, 1)
        return (d_query, d_keys, d_values)

    full_zeros = jnp.zeros((SEQS, seq_len, local_width), jnp.float32)
    d_query, d_keys, d_values = lax.fori_loop(
        0, block_count, full_grad, (zeros_q, full_zeros, full_zeros)
    )
    d_key_own, d_value_own = (
        lax.psum_scatter(d_keys, "ctx", scatter_dimension=1, tiled=True),
        lax.psum_scatter(d_values, "ctx", scatter_dimension=1, tiled=True),
    )
    grad_shape = (SEQS, tok_seq, heads_here, HD)
    return (
        attended,
        d_query * score_scale,
        d_key_own.reshape(grad_shape) * score_scale,
        d_value_own.reshape(grad_shape),
    )


def head_kernel(score_scale, table, x_ref, y_ref, sorted_rows, turned, key_value, sorted_out):
    length = x_ref.shape[0]
    for run in range(length // RUN):
        place = pl.multiple_of(table[run] * RUN, RUN)
        sorted_rows[pl.ds(place, RUN), :] = x_ref[run * RUN : (run + 1) * RUN, :]
    for start in range(0, length, TILE):
        chunk = sorted_rows[start : start + TILE, :].astype(jnp.float32)
        turned[:, start : start + TILE] = chunk.T.astype(jnp.bfloat16)
    key_value[...] = jnp.zeros_like(key_value)

    def multiply(left_side, right_side):
        return jnp.dot(left_side, right_side, preferred_element_type=jnp.float32)

    key_index = lax.broadcasted_iota(jnp.int32, (TILE, TILE), 0)
    query_index = lax.broadcasted_iota(jnp.int32, (TILE, TILE), 1)
    allowed = key_index <= query_index
    for start in range(0, length, TILE):
        width = start + TILE
        tile = slice(start, width)
        query_tile = sorted_rows[tile, :HD]
        key_rows = sorted_rows[:width, HD : 2 * HD]
        value_rows = sorted_rows[:width, 2 * HD : 3 * HD]
        scores = multiply(key_rows, turned[:HD, tile])
        edge = jnp.where(allowed, scores[start:, :], MASKED_SCORE)
        scores = edge if start == 0 else jnp.concatenate([scores[:start, :], edge], axis=0)
        top = jnp.max(scores, axis=0, keepdims=True)
        exp_terms = jnp.exp(scores - top)
        total = jnp.sum(exp_terms, axis=0, keepdims=True)
        weights = exp_terms.astype(jnp.bfloat16)
        numerator = multiply(turned[2 * HD : 3 * HD, :width], weights)
        d_att = turned[3 * HD :, tile].astype(jnp.float32)
        d_numer = d_att / total
        corr = jnp.sum(d_att * numerator, axis=0, keepdims=True) / (total * total)
        along_value = multiply(value_rows, d_numer.astype(jnp.bfloat16))
        d_score = (exp_terms * (along_value - corr)).astype(jnp.bfloat16)
        d_query = multiply(turned[HD : 2 * HD, :width], d_score) * score_scale
        both = jnp.concatenate([d_query, numerator / total], axis=0)
        sorted_out[tile, : 2 * HD] = both.T.astype(jnp.bfloat16)
        key_value[:width, :HD] += multiply(d_score, query_tile)
        key_value[:width, HD:] += multiply(weights, d_numer.T.astype(jnp.bfloat16))
    sorted_out[:, 2 * HD :] = key_value[...].astype(jnp.bfloat16)
    for run in range(length // RUN):
        place = pl.multiple_of(table[run] * RUN, RUN)
        y_ref[run * RUN : (run + 1) * RUN, :] = sorted_out[pl.ds(place, RUN), :]


def head_attention(packed, table, score_scale):
    length, width = packed.shape
    pairs = length * length // 2
    return pl.pallas_call(
        partial(head_kernel, score_scale),
        out_shape=jax.ShapeDtypeStruct((length, width), jnp.bfloat16),
        in_specs=[
            pl.BlockSpec(memory_space=pltpu.SMEM),
            pl.BlockSpec(memory_space=pltpu.VMEM),
        ],
        out_specs=pl.BlockSpec(memory_space=pltpu.VMEM),
        scratch_shapes=[
            pltpu.VMEM((length, width), jnp.bfloat16),
            pltpu.VMEM((width, length), jnp.bfloat16),
            pltpu.VMEM((length, 2 * HD), jnp.float32),
            pltpu.VMEM((length, width), jnp.bfloat16),
        ],
        compiler_params=pltpu.CompilerParams(vmem_limit_bytes=48 * 1024 * 1024),
        cost_estimate=pl.CostEstimate(
            flops=12 * pairs * HD, bytes_accessed=4 * length * width, transcendentals=pairs
        ),
    )(table, packed)


def swap_with(array, bit, axis_name="ctx"):
    count = lax.axis_size(axis_name)
    return lax.ppermute(array, axis_name, [(index, index ^ bit) for index in range(count)])


def sum_halves(partial_sum, bits):
    here = lax.axis_index("ctx")
    held = partial_sum
    for bit in bits:
        half = held.shape[0] // 2
        side = jnp.where((here & bit) != 0, 1, 0)
        sent = lax.dynamic_slice_in_dim(held, (1 - side) * half, half, 0).astype(jnp.bfloat16)
        kept = lax.dynamic_slice_in_dim(held, side * half, half, 0)
        held = kept + swap_with(sent, bit).astype(jnp.float32)
    return held.astype(jnp.bfloat16)


def join_halves(held, bits):
    here = lax.axis_index("ctx")
    for bit in reversed(bits):
        other = swap_with(held, bit)
        upper = (here & bit) != 0
        held = jnp.concatenate(
            [jnp.where(upper, other, held), jnp.where(upper, held, other)], axis=0
        )
    return held.astype(jnp.float32)


def sum_small(values, axis_name):
    bit = 1
    while bit < lax.axis_size(axis_name):
        values = values + swap_with(values, bit, axis_name)
        bit *= 2
    return values


def scatter_cols(partial_sum):
    count = lax.axis_size("tp")
    here = lax.axis_index("tp")
    rows, width = partial_sum.shape
    col_count = width // count
    held = [partial_sum[:, index * col_count : (index + 1) * col_count] for index in range(count)]
    bit = 1
    while bit < count:
        upper = (here & bit) != 0
        pairs = list(zip(held[::2], held[1::2]))
        sent = jnp.concatenate([jnp.where(upper, low, high) for low, high in pairs], axis=0)
        other = swap_with(sent.astype(jnp.bfloat16), bit, "tp").astype(jnp.float32)
        held = [
            jnp.where(upper, high, low) + other[index * rows : (index + 1) * rows]
            for index, (low, high) in enumerate(pairs)
        ]
        bit *= 2
    return held[0]


def bit_orders(count):
    bits = []
    while 1 << len(bits) < count:
        bits.append(1 << len(bits))
    return (bits, bits[1:2] + bits[:1] + bits[2:])


def local(
    inputs,
    cotangent,
    positions,
    first_gain,
    first_shift,
    second_gain,
    second_shift,
    qkv_weight,
    qkv_bias,
    dense_weight,
    dense_bias,
    up_weight,
    up_bias,
    down_weight,
    down_bias,
):
    ctx_count = lax.axis_size("ctx")
    tp_count = lax.axis_size("tp")
    ctx_here = lax.axis_index("ctx")
    tp_here = lax.axis_index("tp")
    tok_dev, model_width = inputs.shape
    tok_seq = tok_dev // SEQS
    local_width = dense_weight.shape[0]
    heads_here = local_width // HD
    seq_len = tok_seq * ctx_count
    block_len = min(2048, seq_len)
    block_count = seq_len // block_len
    score_scale = HD ** (-0.5)
    col_count = model_width // tp_count
    place_grid = positions.reshape(ctx_count, SEQS, tok_seq)
    own_places = lax.dynamic_index_in_dim(place_grid, ctx_here, 0, keepdims=False)
    all_places = jnp.transpose(place_grid, (1, 0, 2)).reshape(SEQS, seq_len)

    def take_cols(array):
        return lax.dynamic_slice_in_dim(array, tp_here * col_count, col_count, array.ndim - 1)

    input_rows = inputs.astype(jnp.float32)
    normed_one = layer_norm(input_rows, first_gain, first_shift).astype(jnp.bfloat16)
    qkv_mixed = (
        jnp.einsum("td,dce->tce", normed_one, qkv_weight, preferred_element_type=jnp.float32)
        + qkv_bias
    )
    qkv_split = qkv_mixed.reshape(SEQS, tok_seq, 3, heads_here, HD)
    queries = rotate(qkv_split[:, :, 0], own_places, ROT).astype(jnp.bfloat16)
    key_own = rotate(qkv_split[:, :, 1], own_places, ROT).astype(jnp.bfloat16)
    value_own = qkv_split[:, :, 2].astype(jnp.bfloat16)
    d_att = contract_cols(cotangent, dense_weight).reshape(SEQS, tok_seq, heads_here, HD)
    orders = bit_orders(ctx_count)
    one_head = ctx_count == SEQS * heads_here and seq_len % TILE == 0 and tok_seq % RUN == 0
    if one_head:
        packed = jnp.stack(
            [
                (queries * score_scale).astype(jnp.bfloat16),
                key_own,
                value_own,
                d_att.astype(jnp.bfloat16),
            ],
            axis=3,
        )
        packed = jnp.transpose(packed, (0, 2, 1, 3, 4)).reshape(ctx_count, tok_seq, 4 * HD)
        packed, inputs = lax.optimization_barrier((packed, inputs))
        packed = lax.all_to_all(packed, "ctx", 0, 0, tiled=True).reshape(seq_len, 4 * HD)

    input_rows = inputs.astype(jnp.float32)
    normed_two = layer_norm(input_rows, second_gain, second_shift).astype(jnp.bfloat16)
    up_proj = jnp.dot(normed_two, up_weight, preferred_element_type=jnp.float32) + up_bias
    activated = jax.nn.gelu(up_proj, approximate=False).astype(jnp.bfloat16)
    cot_rows = cotangent.astype(jnp.float32)
    gelu_pull = jax.vjp(partial(jax.nn.gelu, approximate=False), up_proj)[1]
    d_up = gelu_pull(contract_cols(cotangent, down_weight))[0].astype(jnp.bfloat16)
    half_down = sum_halves(contract_rows(activated, cotangent), orders[0])
    half_up = sum_halves(contract_rows(normed_two, d_up), orders[1])
    grad_up_bias = jnp.sum(d_up.astype(jnp.float32), axis=0)
    d_two = contract_cols(d_up, up_weight)
    two_cols = scatter_cols(d_two)

    if one_head:
        starts = lax.dynamic_index_in_dim(place_grid, ctx_here // heads_here, 1, keepdims=False)
        table = starts.reshape(seq_len // RUN, RUN)[:, 0] // RUN
        grads = head_attention(packed, table, score_scale).reshape(ctx_count, tok_seq, 4 * HD)
        grads = lax.all_to_all(grads, "ctx", 0, 0, tiled=True)
        grads = grads.reshape(SEQS, heads_here, tok_seq, 4, HD)
        grads = jnp.transpose(grads, (3, 0, 2, 1, 4))
        attended = grads[1].reshape(tok_dev, local_width)
        d_query, d_key_own, d_value_own = (
            grads[0].astype(jnp.float32),
            grads[2].astype(jnp.float32),
            grads[3].astype(jnp.float32),
        )
    else:
        attended, d_query, d_key_own, d_value_own = spread_attention(
            queries,
            key_own,
            value_own,
            d_att,
            own_places,
            all_places,
            block_len,
            block_count,
            score_scale,
        )

    zeros_q = jnp.zeros((SEQS, tok_seq, heads_here, HD), jnp.float32)
    turn_back = jax.vjp(partial(rotate, places=own_places, rot_dims=ROT), zeros_q)[1]
    d_mixed = jnp.stack(
        [turn_back(d_query)[0], turn_back(d_key_own)[0], d_value_own], axis=2
    )
    d_mixed = d_mixed.reshape(tok_dev, 3, local_width).astype(jnp.bfloat16)
    grad_qkv = contract_rows(normed_one, d_mixed.reshape(tok_dev, 3 * local_width))
    grad_dense = contract_rows(cotangent, attended)
    joined = jnp.concatenate([grad_qkv, grad_dense], axis=1)
    half_down, half_up, joined = lax.optimization_barrier((half_down, half_up, joined))
    grad_down = join_halves(half_down, orders[0])
    grad_up = join_halves(half_up, orders[1])
    middle = model_width // 2
    joined = jnp.concatenate(
        [
            join_halves(sum_halves(joined[:middle], orders[0]), orders[0]),
            join_halves(sum_halves(joined[middle:], orders[1]), orders[1]),
        ],
        axis=0,
    )
    grad_qkv = joined[:, : 3 * local_width].reshape(model_width, 3, local_width)
    grad_dense = joined[:, 3 * local_width :].T
    grad_qkv_bias = jnp.sum(d_mixed.astype(jnp.float32), axis=0)
    d_one = jnp.einsum("tce,dce->td", d_mixed, qkv_weight, preferred_element_type=jnp.float32)
    partial_out = jnp.dot(attended, dense_weight, preferred_element_type=jnp.float32) + jnp.dot(
        activated, down_weight, preferred_element_type=jnp.float32
    )
    scattered = scatter_cols(jnp.concatenate([partial_out, d_one], axis=0))
    summed, one_cols = (scattered[:tok_dev], scattered[tok_dev:])
    output = (take_cols(input_rows) + summed + take_cols(dense_bias) + take_cols(down_bias)).astype(
        jnp.bfloat16
    )

    centered = input_rows - jnp.mean(input_rows, axis=-1, keepdims=True)
    inverse_spread = lax.rsqrt(jnp.mean(centered * centered, axis=-1, keepdims=True) + EPSILON)
    normalized = centered * inverse_spread
    scaled_one = d_one * first_gain
    scaled_two = d_two * second_gain
    means = sum_small(
        jnp.stack(
            [
                jnp.mean(scaled_one + scaled_two, axis=-1),
                jnp.mean((scaled_one + scaled_two) * normalized, axis=-1),
            ]
        ),
        "tp",
    )
    cols = take_cols(normalized)
    scaled_cols = one_cols * take_cols(first_gain) + two_cols * take_cols(second_gain)
    d_rows = take_cols(cot_rows) + inverse_spread * (
        scaled_cols - means[0][:, None] - cols * means[1][:, None]
    )
    small = jnp.concatenate(
        [
            jnp.sum(one_cols * cols, axis=0),
            jnp.sum(one_cols, axis=0),
            jnp.sum(two_cols * cols, axis=0),
            jnp.sum(two_cols, axis=0),
            grad_qkv_bias.reshape(-1),
            jnp.sum(cot_rows, axis=0),
            grad_up_bias,
        ]
    )
    small = sum_small(small, "ctx")
    gains = [small[index * col_count : (index + 1) * col_count] for index in range(4)]
    small = small[4 * col_count :]
    grad_qkv_bias = small[: 3 * local_width].reshape(3, local_width)
    small = small[3 * local_width :]
    bias_grad = small[:model_width]
    return (
        output,
        d_rows,
        *gains,
        grad_qkv,
        grad_qkv_bias,
        grad_dense,
        bias_grad,
        grad_up,
        small[model_width:],
        grad_down,
        bias_grad,
    )


def solution(mesh):
    in_specs = (
        P("ctx", None),
        P("ctx", None),
        P(),
        P(),
        P(),
        P(),
        P(),
        P(None, None, "tp"),
        P(None, "tp"),
        P("tp", None),
        P(),
        P(None, "tp"),
        P("tp"),
        P("tp", None),
        P(),
    )
    out_specs = (
        P("ctx", "tp"),
        P("ctx", "tp"),
        P("tp"),
        P("tp"),
        P("tp"),
        P("tp"),
        P(None, None, "tp"),
        P(None, "tp"),
        P("tp", None),
        P(),
        P(None, "tp"),
        P("tp"),
        P("tp", None),
        P(),
    )
    return jax.shard_map(local, mesh=mesh, in_specs=in_specs, out_specs=out_specs, check_vma=False)
```
